32 devices in a mesh: group: 2 (over x), slab: 16 (over z, y, core).
Axes of the slice: x: 2, y: 2, z: 4, core: 2. Of those that a mesh axis runs over, the one named last changes fastest.
Arguments:
- field: float32 [4, 64, 64, 4096], P('group', 'slab'), parts along dimension 0, may hold values from -6 to 6
- out_grad: float32 [4, 64, 64, 4096], P('group', 'slab'), parts along dimension 0, may hold values from -6 to 6
- kept: int32 [48], replicated, may hold values from 0 to 511, as said below
- mixing: float32 [48, 32, 64, 128], P('slab'), may hold values from -3 to 3
Outputs:
- grad_mixing: float32 [96, 32, 64, 128], P(('group', 'slab')), parts along dimension 0
- grad_field: float32 [4, 64, 64, 4096], P('group', 'slab'), parts along dimension 0
The draws below stay inside these ranges and needn't reach their ends.
There are 2 independent parts, one for each index of `group`. The reference program is written for one: setup_inputs(seed, part) draws one part's arguments, and reference() takes and returns one part's arrays. A program takes and returns all parts, laid end to end along the dimension named above; an argument that names none is the same for every part. Nothing has to cross between parts.
Inputs may be any that keep to these rules, and one draw needn't show every extreme that they name: `kept`: 48 distinct pencil indices; pencil 0 and pencil 32 * 16 - 1 are always among them.
All inputs are finite; a program needn't handle non-finite values.
Results may differ from the reference program's by a relative error of at most 0.00011.
Values sent between devices are 32-bit elements; how exact they have to be, the bound alone decides.
A program may use at most 128 MiB of HBM per device.

```python
import math
import jax
import jax.numpy as jnp
from jax import lax

NX = 64
NY = 64
NZ = 64
C = 64
KX = 32
KY = 32
KZ = 16
SAMPLES = 2
KEPT = 48


def draw_kept(key, part):
    total = KY * KZ
    first, second = jax.random.split(key)
    inner = (jax.random.permutation(first, total - 2) + 1).astype(jnp.int32)
    chosen = jnp.concatenate([jnp.array([0, total - 1], dtype=jnp.int32), inner[:KEPT - 2]])
    order = jax.random.permutation(second, KEPT)
    return chosen[order].astype(jnp.int32)


def block_levels(rng, extent, cuts, low, top_value):
    level = 1.0
    for axis_at, blocks in cuts:
        steps = jax.random.uniform(jax.random.fold_in(jax.random.fold_in(rng, 6), axis_at), (blocks,), jnp.float32, low / len(cuts), top_value / len(cuts))
        level = level * jnp.repeat(jnp.exp(steps), extent[axis_at] // blocks).reshape((-1,) + (1,) * (len(extent) - 1 - axis_at))
    return level


def gaussian(rng, dims, scale, reach, cuts=(), held_as=jnp.bfloat16):
    values = scale * jax.random.normal(rng, dims, jnp.float32)
    if cuts:
        values = values * block_levels(rng, dims, cuts, -0.22, 0.18)
    return jnp.clip(values, -reach, reach).astype(held_as)


def setup_inputs(seed: int = 0, part: int = 0) -> dict:
    key_list = jax.random.split(jax.random.key(seed), 5)
    part_splits = jax.random.split(jax.random.fold_in(key_list[4], part), 5)
    field = gaussian(part_splits[0], (SAMPLES, NX, C, NY * NZ), 1.0, 6.0, ((1, 16),), jnp.float32)
    out_grad = gaussian(part_splits[1], (SAMPLES, NX, C, NY * NZ), 1.0, 6.0, ((1, 16),), jnp.float32)
    kept = draw_kept(jax.random.fold_in(key_list[4], 71), part)
    mixing = gaussian(key_list[3], (KEPT, KX, C, 2 * C), 0.5, 3.0, ((0, 16),), jnp.float32)
    return dict(field=field, out_grad=out_grad, kept=kept, mixing=mixing)


HIGH = lax.Precision.HIGHEST

def signed_modes(index, count):
    return jnp.where(index < count // 2, index, index - count)

def plane_tables(kept):
    freq_y = signed_modes(kept // KZ, KY)
    freq_z = kept % KZ
    cells = jnp.arange(NY * NZ, dtype=jnp.int32)
    along_y = cells // NZ
    along_z = cells % NZ
    turn_y = along_y[:, None] * freq_y[None, :] % NY
    turn_z = along_z[:, None] * freq_z[None, :] % NZ
    angle = turn_y.astype(jnp.float32) * (2.0 * math.pi / NY) + turn_z.astype(jnp.float32) * (2.0 * math.pi / NZ)
    return (jnp.cos(angle), jnp.sin(angle))

def line_tables():
    freq_x = signed_modes(jnp.arange(KX, dtype=jnp.int32), KX)
    rows = jnp.arange(NX, dtype=jnp.int32)
    turn = rows[:, None] * freq_x[None, :] % NX
    angle = turn.astype(jnp.float32) * (2.0 * math.pi / NX)
    return (jnp.cos(angle), jnp.sin(angle))

def scale_all():
    return 1.0 / math.sqrt(NX * NY * NZ)

def plane_forward(values, plane_cos, plane_sin):
    real = jnp.einsum('bxcq,qp->pbxc', values, plane_cos, precision=HIGH)
    imag = -jnp.einsum('bxcq,qp->pbxc', values, plane_sin, precision=HIGH)
    return jnp.concatenate([real, imag], axis=3)

def line_forward(spec, line_cos, line_sin):
    width = spec.shape[3] // 2
    first = jnp.einsum('pbxk,xa->pbak', spec, line_cos, precision=HIGH)
    second = jnp.einsum('pbxk,xa->pbak', spec, line_sin, precision=HIGH)
    real = first[..., :width] + second[..., width:]
    imag = first[..., width:] - second[..., :width]
    return scale_all() * jnp.concatenate([real, imag], axis=3)

def line_inverse(modes, line_cos, line_sin):
    width = modes.shape[3] // 2
    first = jnp.einsum('pbak,xa->pbxk', modes, line_cos, precision=HIGH)
    second = jnp.einsum('pbak,xa->pbxk', modes, line_sin, precision=HIGH)
    real = first[..., :width] - second[..., width:]
    imag = second[..., :width] + first[..., width:]
    return jnp.concatenate([real, imag], axis=3)

def plane_inverse(lines, plane_cos, plane_sin):
    width = lines.shape[3] // 2
    real = jnp.einsum('pbxc,qp->bxcq', lines[..., :width], plane_cos, precision=HIGH)
    imag = jnp.einsum('pbxc,qp->bxcq', lines[..., width:], plane_sin, precision=HIGH)
    return scale_all() * (real - imag)

def mix_modes(modes, mixing):
    width = mixing.shape[2]
    first = jnp.einsum('pbai,paio->pbao', modes[..., :width], mixing, precision=HIGH)
    second = jnp.einsum('pbai,paio->pbao', modes[..., width:], mixing, precision=HIGH)
    real = first[..., :width] - second[..., width:]
    imag = first[..., width:] + second[..., :width]
    return jnp.concatenate([real, imag], axis=3)

def weight_grad(modes, grads):
    width = grads.shape[3] // 2
    first = jnp.einsum('pbai,pbao->paio', modes[..., :width], grads, precision=HIGH)
    second = jnp.einsum('pbai,pbao->paio', modes[..., width:], grads, precision=HIGH)
    real = first[..., :width] + second[..., width:]
    imag = first[..., width:] - second[..., :width]
    return jnp.concatenate([real, imag], axis=3)

def input_grad(mixing, grads):
    width = mixing.shape[2]
    w_real = mixing[..., :width]
    w_imag = mixing[..., width:]
    g_real = grads[..., :width]
    g_imag = grads[..., width:]
    real = jnp.einsum('paio,pbao->pbai', w_real, g_real, precision=HIGH) + jnp.einsum('paio,pbao->pbai', w_imag, g_imag, precision=HIGH)
    imag = jnp.einsum('paio,pbao->pbai', w_real, g_imag, precision=HIGH) - jnp.einsum('paio,pbao->pbai', w_imag, g_real, precision=HIGH)
    return jnp.concatenate([real, imag], axis=3)

def gelu_slope(pre):
    return 0.5 * (1.0 + lax.erf(pre * (1.0 / math.sqrt(2.0)))) + pre * jnp.exp(-0.5 * pre * pre) * (1.0 / math.sqrt(2.0 * math.pi))

def reference(field, out_grad, kept, mixing):
    plane_cos, plane_sin = plane_tables(kept)
    line_cos, line_sin = line_tables()
    factor = jnp.where(kept % KZ > 0, 2.0, 1.0).astype(jnp.float32)[:, None, None, None]
    modes_u = line_forward(plane_forward(field, plane_cos, plane_sin), line_cos, line_sin)
    mixed = factor * mix_modes(modes_u, mixing)
    pre = plane_inverse(line_inverse(mixed, line_cos, line_sin), plane_cos, plane_sin)
    grad_pre = out_grad * gelu_slope(pre)
    grad_spec = factor * line_forward(plane_forward(grad_pre, plane_cos, plane_sin), line_cos, line_sin)
    grad_mixing = weight_grad(modes_u, grad_spec)
    spectrum_du = input_grad(mixing, grad_spec)
    grad_field = plane_inverse(line_inverse(spectrum_du, line_cos, line_sin), plane_cos, plane_sin)
    return (grad_mixing, grad_field)
```

```python
import functools
import math

import jax
import jax.numpy as jnp
from jax import lax
from jax.experimental import pallas as pl
from jax.experimental.pallas import tpu as pltpu
from jax.sharding import PartitionSpec as P

NX = 64
NY = 64
NZ = 64
KX = 32
KY = 32
KZ = 16
CELLS = NY * NZ
C = 64
LANES = 2 * C
UNIT = 2.0 * math.pi / 64
SCALE = 1.0 / math.sqrt(NX * NY * NZ)
HIGH = lax.Precision.HIGHEST
F32 = jnp.float32
BF16 = jnp.bfloat16
MESH = pl.DeviceIdType.MESH


def split(v):
    hi = v.astype(BF16)
    return hi, (v - hi.astype(F32)).astype(BF16)


def dot(a, b):
    return jnp.dot(a, b, preferred_element_type=F32)


def iota(shape, dim):
    return lax.broadcasted_iota(jnp.int32, shape, dim)


def freqs(kept):
    ky = lax.div(kept, KZ)
    fy = jnp.where(ky < KY // 2, ky, ky - KY)
    return fy, lax.rem(kept, KZ)


def turns(count):
    return (count & 63).astype(F32) * UNIT


def build_rows(kept, table, rows):
    fy, fz = freqs(kept)
    lane = iota((rows, LANES), 1)
    phase = (iota((rows, LANES), 0) & 1) * 16
    used = (kept >= 0).astype(F32)
    base = turns(fy * (lane >> 6) + fz * (lane & 63) + phase)
    step = turns(2 * fy)
    sc, ss = jnp.cos(step), jnp.sin(step)

    def body(t, carry):
        c, s = carry
        hi, lo = split(c)
        at = pl.ds(pl.multiple_of(t * LANES, LANES), LANES)
        table[pl.ds(0, rows), at] = hi
        table[pl.ds(rows, rows), at] = lo
        return c * sc - s * ss, s * sc + c * ss

    lax.fori_loop(0, CELLS // LANES, body, (jnp.cos(base) * used, jnp.sin(base) * used))


def build_columns(kept, table, rows):
    kept = jnp.broadcast_to(kept, (NZ, rows))
    fy, fz = freqs(kept)
    phase = (iota((NZ, rows), 1) & 1) * 16
    used = (kept >= 0).astype(F32)
    base = turns(fz * iota((NZ, rows), 0) + phase)
    step = turns(fy)
    sc, ss = jnp.cos(step), jnp.sin(step)

    def body(t, carry):
        c, s = carry
        hi, lo = split(c)
        at = pl.ds(pl.multiple_of(t * NZ, NZ), NZ)
        table[at, pl.ds(0, rows)] = hi
        table[at, pl.ds(rows, rows)] = lo
        return c * sc - s * ss, s * sc + c * ss

    lax.fori_loop(0, NY, body, (jnp.cos(base) * used, jnp.sin(base) * used))


def x_of(index, n, planes):
    return lax.rem(index, n) * planes + lax.div(index, n)


def signed_x(a):
    return jnp.where(a < KX // 2, a, a - KX)


def swap(v):
    return pltpu.roll(v, C, 1)


def gelu_slope(v):
    a = jnp.abs(v)
    t = 1.0 / (1.0 + a * (0.3275911 / math.sqrt(2.0)))
    tail = t * (0.127414796 + t * (-0.142248368 + t * (0.7107068705 + t * (-0.7265760135 + t * 0.5307027145))))
    over = 1.0 + jnp.exp(-0.5 * v * v) * (a * (1.0 / math.sqrt(2.0 * math.pi)) - tail)
    return jnp.where(v >= 0, over, 1.0 - over)


def lines_matrix(got, b, store, n, planes, owned):
    for x in range(planes):
        for g in range(2 * owned):
            store[:, g, pl.ds(x * C, C)] = got[b, :, x, pl.ds(g * C, C)]
    lines = store[...].reshape(n * 8, planes * C).T
    hi, lo = split(lines)
    return jnp.concatenate([hi, hi], axis=1), lo


def main_kernel(
    n, planes, owned,
    kept_s, kept_r, kept_c, field, out_grad, mixing,
    modes_out, grads_out, lines_out,
    f_v, o_v, w_v, w_b, t_r, t_c, acc, store, left, res, mid, send, recv,
    f_sem, o_sem, w_sem, send_sem, recv_sem, out_sem,
):
    rows = n * 8
    samples = f_v.shape[0]
    chunks = f_sem.shape[1]
    width = CELLS // chunks
    me = lax.axis_index("slab")
    barrier = pltpu.get_barrier_semaphore()

    def greet(k, _):
        pl.semaphore_signal(barrier, inc=1, device_id={"slab": lax.rem(me + k, n)}, device_id_type=MESH)
        return 0

    lax.fori_loop(1, n, greet, 0)

    def load(src, dst, sem, b, k):
        at = pl.ds(k * width, width)
        return pltpu.make_async_copy(src.at[b, :, :, at], dst.at[b, :, :, at], sem.at[b, k])

    w_load = pltpu.make_async_copy(mixing, w_v, w_sem)
    for b in range(samples):
        for k in range(chunks):
            load(field, f_v, f_sem, b, k).start()
    w_load.start()
    for b in range(samples):
        for k in range(chunks):
            load(out_grad, o_v, o_sem, b, k).start()

    build_columns(kept_c[0:1, :], t_c, rows)

    turn = signed_x(iota((KX, NX), 0)) * x_of(iota((KX, NX), 1), n, planes)
    to_modes = jnp.concatenate([jnp.cos(turns(turn)), jnp.sin(turns(turn))], axis=0)
    turn = signed_x(iota((NX, KX), 1)) * x_of(iota((NX, KX), 0), n, planes)
    to_lines = jnp.concatenate([jnp.cos(turns(turn)), jnp.sin(turns(turn))], axis=0)
    sign = jnp.where(iota((KX, LANES), 1) < C, 1.0, -1.0).astype(F32)
    sign_x = jnp.where(iota((NX, LANES), 1) < C, -1.0, 1.0).astype(F32)

    def factor(j):
        kept = kept_s[me * owned + j]
        return jnp.where(lax.rem(kept, KZ) > 0, 2.0, 1.0).astype(F32) * SCALE

    factors = [factor(j) for j in range(owned)]

    def exchange(phase, b):
        def go(k, _):
            to = lax.rem(me + k, n)
            pltpu.make_async_remote_copy(
                src_ref=send.at[phase, b, to],
                dst_ref=recv.at[phase, b, me],
                send_sem=send_sem.at[phase, b],
                recv_sem=recv_sem.at[phase, b],
                device_id={"slab": to},
                device_id_type=MESH,
            ).start()
            return 0

        lax.fori_loop(1, n, go, 0)
        recv[phase, b, me] = send[phase, b, me]

    def arrive(phase, b):
        part = recv.at[phase, b, pl.ds(0, n - 1)]
        pltpu.make_async_copy(part, part, recv_sem.at[phase, b]).wait()

    def spread(phase, b):
        store[...] = acc[...].T.reshape(n, 8, planes * C)
        for x in range(planes):
            pieces = [store[:, g, pl.ds(x * C, C)] for g in range(2 * owned)]
            send[phase, b, :, x, :] = jnp.concatenate(pieces, axis=1)

    def plane_products(v, at):
        hi, lo = split(v)
        first = dot(hi, t_c[at, :])
        return first[:, :rows] + first[:, rows:] + dot(lo, t_c[at, pl.ds(0, rows)])

    def forward_field(b):
        for k in range(chunks):
            load(field, f_v, f_sem, b, k).wait()
            v = f_v[b, :, :, pl.ds(k * width, width)].reshape(planes * C, width)
            got = plane_products(v, pl.ds(k * width, width))
            acc[...] = got if k == 0 else acc[...] + got

    def received_modes(phase, b):
        lines = jnp.concatenate([recv[phase, b, :, x, :] for x in range(planes)], axis=0)
        both = jnp.dot(to_modes, lines, preferred_element_type=F32, precision=HIGH)
        out = []
        for j in range(owned):
            at = slice(j * LANES, (j + 1) * LANES)
            out.append(both[:KX, at] + swap(both[KX:, at]) * sign)
        return out

    def products(transposed):
        dims = (((1,), (1 if transposed else 0,)), ((), ()))

        def body(i, _):
            for u in range(8):
                at = i * 8 + u
                res[at] = lax.dot_general(left[at].astype(BF16), w_b[at], dims, preferred_element_type=F32)
            return 0

        lax.fori_loop(0, owned * KX // 8, body, 0)

    def send_lines(phase, b, modes):
        modes = jnp.concatenate(modes, axis=1)
        both = jnp.dot(to_lines, modes, preferred_element_type=F32, precision=HIGH)
        out = []
        for j in range(owned):
            at = slice(j * LANES, (j + 1) * LANES)
            out.append(both[:NX, at] + swap(both[NX:, at]) * sign_x)
        lines = jnp.concatenate(out, axis=1)
        for x in range(planes):
            send[phase, b, :, x, :] = lines[x * n : (x + 1) * n, :]
        exchange(phase, b)

    low = iota((KX, LANES), 1) < C

    def mix(b):
        for j, modes in enumerate(received_modes(0, b)):
            modes = modes * SCALE
            mid[0, j, b] = modes
            hi = modes.astype(BF16).astype(F32)
            lo = (modes - hi).astype(BF16).astype(F32)
            at = pl.ds(j * KX, KX)
            left[at, 0, :] = jnp.where(low, hi, swap(hi))
            left[at, 1, :] = jnp.where(low, swap(hi), hi)
            left[at, 2, :] = jnp.where(low, lo, 0.0)
            left[at, 3, :] = jnp.where(low, swap(lo), 0.0)
        products(False)
        out = []
        for j in range(owned):
            at = pl.ds(j * KX, KX)
            first = res[at, 0, :] + res[at, 2, :]
            second = res[at, 1, :] + res[at, 3, :]
            out.append((first - swap(second) * sign) * factors[j])
        send_lines(1, b, out)

    def unmix(b):
        for j, grads in enumerate(received_modes(2, b)):
            grads = grads * factors[j]
            mid[1, j, b] = grads
            hi = grads.astype(BF16).astype(F32)
            lo = (grads - hi).astype(BF16).astype(F32)
            at = pl.ds(j * KX, KX)
            left[at, 0, :] = hi
            left[at, 1, :] = swap(hi) * sign
            left[at, 2, :] = lo
            left[at, 3, :] = swap(lo) * sign
        products(True)
        out = []
        for j in range(owned):
            at = pl.ds(j * KX, KX)
            real_hi, imag_hi = res[at, 0, :], res[at, 1, :]
            real = real_hi + swap(real_hi) + res[at, 2, :]
            imag = imag_hi + swap(imag_hi) + res[at, 3, :]
            out.append(jnp.where(low, real, swap(imag)) * SCALE)
        send_lines(3, b, out)

    def through_cells(b):
        first, second = lines_matrix(recv.at[1], b, store, n, planes, owned)
        for k in range(chunks):
            load(out_grad, o_v, o_sem, b, k).wait()
        acc[...] = jnp.zeros_like(acc)
        step = 256

        def body(k, _):
            at = pl.ds(pl.multiple_of(k * step, step), step)
            pre = dot(first, t_r[:, at]) + dot(second, t_r[pl.ds(0, rows), at])
            v = o_v[b, :, :, at].reshape(planes * C, step) * gelu_slope(pre)
            acc[...] += plane_products(v, at)
            return 0

        lax.fori_loop(0, CELLS // step, body, 0)

    forward_field(0)
    spread(0, 0)
    pl.semaphore_wait(barrier, n - 1)
    exchange(0, 0)
    for b in range(1, samples):
        forward_field(b)
        spread(0, b)
        exchange(0, b)

    build_rows(kept_r[...], t_r, rows)
    left[...] = jnp.zeros_like(left)
    w_load.wait()

    def cut(i, _):
        hi, lo = split(w_v[i])
        w_b[i, pl.ds(0, C), :] = hi
        w_b[i, pl.ds(C, C), :] = lo
        return 0

    lax.fori_loop(0, owned * KX, cut, 0)

    for b in range(samples):
        arrive(0, b)
        mix(b)
    store[...] = jnp.zeros_like(store)
    for b in range(samples):
        arrive(1, b)
        through_cells(b)
        spread(2, b)
        exchange(2, b)
    for b in range(samples):
        arrive(2, b)
        unmix(b)
    outs = [
        pltpu.make_async_copy(mid.at[0], modes_out, out_sem.at[0]),
        pltpu.make_async_copy(mid.at[1], grads_out, out_sem.at[1]),
    ]
    for copy in outs:
        copy.start()
    for b in range(samples):
        arrive(3, b)
    outs.append(pltpu.make_async_copy(recv.at[3], lines_out, out_sem.at[2]))
    outs[2].start()
    for copy in outs:
        copy.wait()
    for phase in range(4):
        for b in range(samples):
            part = send.at[phase, b, pl.ds(0, n - 1)]
            pltpu.make_async_copy(part, part, send_sem.at[phase, b]).wait()


def last_kernel(
    n, planes, owned,
    kept_r, modes, grads, lines,
    gm_out, gf_out,
    t_r, store, lhs, rhs, gm, gf, gm_sem, gf_sem,
):
    rows = n * 8
    samples = gf.shape[0]
    low = iota((KX, LANES), 1) < C
    sign = jnp.where(low, 1.0, -1.0).astype(F32)
    lhs[...] = jnp.zeros_like(lhs)
    rhs[...] = jnp.zeros_like(rhs)
    chunk = KX // 2
    gm_copies = []
    for j in range(owned):
        base = j * KX
        at = pl.ds(base, KX)
        for b in range(samples):
            u, g = modes[j, b], grads[j, b]
            for k, (uu, gg) in enumerate(((u, g), (swap(u), swap(g) * sign))):
                u_hi = uu.astype(BF16).astype(F32)
                u_lo = (uu - u_hi).astype(BF16).astype(F32)
                g_hi = gg.astype(BF16).astype(F32)
                g_lo = (gg - g_hi).astype(BF16).astype(F32)
                row = (b * 2 + k) * 3
                for r, (left, right) in enumerate(((u_hi, g_hi), (u_hi, g_lo), (u_lo, g_hi))):
                    lhs[at, row + r, :] = left
                    rhs[at, row + r, :] = right
    for j in range(owned):
        base = j * KX

        def body(i, _):
            for u in range(4):
                a = base + i * 4 + u
                got = lax.dot_general(
                    lhs[a].astype(BF16), rhs[a].astype(BF16), (((0,), (0,)), ((), ())), preferred_element_type=F32
                )
                gm[a] = got[:C, :]
            return 0

        lax.fori_loop(0, KX // 4, body, 0)
        copy = pltpu.make_async_copy(gm.at[pl.ds(base, KX)], gm_out.at[pl.ds(base, KX)], gm_sem.at[j])
        copy.start()
        gm_copies.append(copy)

    build_rows(kept_r[...], t_r, rows)
    store[...] = jnp.zeros_like(store)
    chunks = gf_sem.shape[1]
    width = CELLS // chunks
    for b in range(samples):
        first, second = lines_matrix(lines, b, store, n, planes, owned)

        def chunk_of(k, b=b):
            at = pl.ds(pl.multiple_of(k * width, width), width)
            return at, pltpu.make_async_copy(gf.at[b, :, :, at], gf_out.at[b, :, :, at], gf_sem.at[b, k])

        def body(k, _):
            at, copy = chunk_of(k)
            out = dot(first, t_r[:, at]) + dot(second, t_r[pl.ds(0, rows), at])
            gf[b, :, :, at] = out.reshape(planes, C, width)
            copy.start()
            return 0

        lax.fori_loop(0, chunks, body, 0)
    for copy in gm_copies:
        copy.wait()
    for b in range(samples):
        def done(k, _, b=b):
            at = pl.ds(pl.multiple_of(k * width, width), width)
            pltpu.make_async_copy(gf.at[b, :, :, at], gf_out.at[b, :, :, at], gf_sem.at[b, k]).wait()
            return 0

        lax.fori_loop(0, chunks, done, 0)


def on_device(n, field, out_grad, kept, mixing):
    samples, planes = field.shape[:2]
    owned = mixing.shape[0]
    rows = n * 8
    kept = kept.astype(jnp.int32)
    each = jnp.broadcast_to(kept.reshape(n, owned, 1), (n, owned, 2)).reshape(n, 2 * owned)
    each = jnp.pad(each, ((0, 0), (0, 8 - 2 * owned)), constant_values=-1).reshape(rows)
    kept_r = jnp.broadcast_to(each[:, None], (rows, LANES))
    kept_c = jnp.broadcast_to(each[None, :], (8, rows))
    vmem = pl.BlockSpec(memory_space=pltpu.VMEM)
    hbm = pl.BlockSpec(memory_space=pl.ANY)
    smem = pl.BlockSpec(memory_space=pltpu.SMEM)
    chunks = 8
    block = (n, planes, owned * LANES)
    modes, grads, lines = pl.pallas_call(
        functools.partial(main_kernel, n, planes, owned),
        out_shape=[
            jax.ShapeDtypeStruct((owned, samples, KX, LANES), F32),
            jax.ShapeDtypeStruct((owned, samples, KX, LANES), F32),
            jax.ShapeDtypeStruct((samples,) + block, F32),
        ],
        in_specs=[smem, vmem, vmem, hbm, hbm, hbm],
        out_specs=[hbm, hbm, hbm],
        scratch_shapes=[
            pltpu.VMEM(field.shape, F32),
            pltpu.VMEM(field.shape, F32),
            pltpu.VMEM((owned * KX, C, LANES), F32),
            pltpu.VMEM((owned * KX, LANES, LANES), BF16),
            pltpu.VMEM((2 * rows, CELLS), BF16),
            pltpu.VMEM((CELLS, 2 * rows), BF16),
            pltpu.VMEM((planes * C, rows), F32),
            pltpu.VMEM((n, 8, planes * C), F32),
            pltpu.VMEM((owned * KX, 8, LANES), F32),
            pltpu.VMEM((owned * KX, 8, LANES), F32),
            pltpu.VMEM((2, owned, samples, KX, LANES), F32),
            pltpu.VMEM((4, samples) + block, F32),
            pltpu.VMEM((4, samples) + block, F32),
            pltpu.SemaphoreType.DMA((samples, chunks)),
            pltpu.SemaphoreType.DMA((samples, chunks)),
            pltpu.SemaphoreType.DMA,
            pltpu.SemaphoreType.DMA((4, samples)),
            pltpu.SemaphoreType.DMA((4, samples)),
            pltpu.SemaphoreType.DMA((3,)),
        ],
        compiler_params=pltpu.CompilerParams(
            collective_id=0, has_side_effects=True, vmem_limit_bytes=56 * 2**20
        ),
    )(kept, kept_r, kept_c, field, out_grad, mixing.reshape(owned * KX, C, LANES))
    grad_mixing, grad_field = pl.pallas_call(
        functools.partial(last_kernel, n, planes, owned),
        out_shape=[
            jax.ShapeDtypeStruct((owned * KX, C, LANES), F32),
            jax.ShapeDtypeStruct(field.shape, F32),
        ],
        in_specs=[vmem, vmem, vmem, vmem],
        out_specs=[hbm, hbm],
        scratch_shapes=[
            pltpu.VMEM((2 * rows, CELLS), BF16),
            pltpu.VMEM((n, 8, planes * C), F32),
            pltpu.VMEM((owned * KX, 16, LANES), F32),
            pltpu.VMEM((owned * KX, 16, LANES), F32),
            pltpu.VMEM((owned * KX, C, LANES), F32),
            pltpu.VMEM(field.shape, F32),
            pltpu.SemaphoreType.DMA((owned,)),
            pltpu.SemaphoreType.DMA((samples, chunks)),
        ],
        compiler_params=pltpu.CompilerParams(vmem_limit_bytes=56 * 2**20),
    )(kept_r, modes, grads, lines)
    return grad_mixing.reshape(mixing.shape), grad_field


def solution(mesh):
    n = mesh.shape["slab"]
    placed = (
        P("group", "slab", None, None),
        P("group", "slab", None, None),
        P(),
        P("slab", None, None, None),
    )
    return jax.shard_map(
        functools.partial(on_device, n),
        mesh=mesh,
        in_specs=placed,
        out_specs=(P(("group", "slab"), None, None, None), P("group", "slab", None, None)),
        check_vma=False,
    )
```

```python
import functools
import math

import jax
import jax.numpy as jnp
from jax import lax
from jax.experimental import pallas as pl
from jax.experimental.pallas import tpu as pltpu
from jax.sharding import PartitionSpec as P

NX = 64
NY = 64
NZ = 64
KX = 32
KY = 32
KZ = 16
CELLS = NY * NZ
C = 64
LANES = 2 * C
UNIT = 2.0 * math.pi / 64
SCALE = 1.0 / math.sqrt(NX * NY * NZ)
HIGH = lax.Precision.HIGHEST
F32 = jnp.float32
BF16 = jnp.bfloat16
MESH = pl.DeviceIdType.MESH


def split(v):
    hi = v.astype(BF16)
    return hi, (v - hi.astype(F32)).astype(BF16)


def dot(a, b):
    return jnp.dot(a, b, preferred_element_type=F32)


def iota(shape, dim):
    return lax.broadcasted_iota(jnp.int32, shape, dim)


def freqs(kept):
    ky = lax.div(kept, KZ)
    fy = jnp.where(ky < KY // 2, ky, ky - KY)
    return fy, lax.rem(kept, KZ)


def turns(count):
    return (count & 63).astype(F32) * UNIT


def build_rows(kept, table, rows):
    fy, fz = freqs(kept)
    lane = iota((rows, LANES), 1)
    phase = (iota((rows, LANES), 0) & 1) * 16
    used = (kept >= 0).astype(F32)
    base = turns(fy * (lane >> 6) + fz * (lane & 63) + phase)
    step = turns(2 * fy)
    sc, ss = jnp.cos(step), jnp.sin(step)

    def body(t, carry):
        c, s = carry
        hi, lo = split(c)
        at = pl.ds(pl.multiple_of(t * LANES, LANES), LANES)
        table[pl.ds(0, rows), at] = hi
        table[pl.ds(rows, rows), at] = lo
        table[pl.ds(2 * rows, rows), at] = hi
        return c * sc - s * ss, s * sc + c * ss

    lax.fori_loop(0, CELLS // LANES, body, (jnp.cos(base) * used, jnp.sin(base) * used))


def build_columns(kept, table, rows):
    kept = jnp.broadcast_to(kept, (NZ, rows))
    fy, fz = freqs(kept)
    phase = (iota((NZ, rows), 1) & 1) * 16
    used = (kept >= 0).astype(F32)
    base = turns(fz * iota((NZ, rows), 0) + phase)
    step = turns(fy)
    sc, ss = jnp.cos(step), jnp.sin(step)

    def body(t, carry):
        c, s = carry
        hi, lo = split(c)
        at = pl.ds(pl.multiple_of(t * NZ, NZ), NZ)
        table[at, pl.ds(0, rows)] = hi
        table[at, pl.ds(rows, rows)] = lo
        return c * sc - s * ss, s * sc + c * ss

    lax.fori_loop(0, NY, body, (jnp.cos(base) * used, jnp.sin(base) * used))


def x_of(index, n, planes):
    return lax.rem(index, n) * planes + lax.div(index, n)


def signed_x(a):
    return jnp.where(a < KX // 2, a, a - KX)


def swap(v):
    return pltpu.roll(v, C, 1)


def gelu_slope(v):
    a = jnp.abs(v)
    d = 1.0 + a * (0.3275911 / math.sqrt(2.0))
    t = pl.reciprocal(d, approx=True)
    t = t * (2.0 - d * t)
    tail = t * (0.127414796 + t * (-0.142248368 + t * (0.7107068705 + t * (-0.7265760135 + t * 0.5307027145))))
    over = jnp.exp2(v * v * (-0.5 / math.log(2.0))) * (a * (1.0 / math.sqrt(2.0 * math.pi)) - tail)
    return jnp.where(v >= 0, 1.0 + over, -over)


def build_spread(table, halves):
    count = table.shape[1]
    k = iota((2 * KX, count), 0) & (KX - 1)
    column = iota((2 * KX, count), 1)
    wanted = column >> 7
    if halves:
        wanted = wanted + ((column >> 6) & 1) * (KX // 2)
    table[...] = jnp.where(k == wanted, 1.0, 0.0).astype(BF16)


def turned(v):
    hi = v.astype(BF16).astype(F32)
    return jnp.concatenate([hi, v - hi], axis=0).T.astype(BF16)


def lines_matrix(got, b, store, n, planes, owned):
    for x in range(planes):
        for g in range(2 * owned):
            store[:, g, pl.ds(x * C, C)] = got[b, :, x, pl.ds(g * C, C)]
    lines = store[...].reshape(n * 8, planes * C).T
    hi, lo = split(lines)
    return jnp.concatenate([hi, hi, lo], axis=1)


def main_kernel(
    n, planes, owned,
    kept_s, kept_r, kept_c, field, out_grad, mixing,
    modes_out, grads_out, lines_out,
    f_v, o_v, w_v, w_t, t_r, t_c, acc, store, pipe, e_mix, e_unmix, res, mid, send, recv,
    f_sem, o_sem, w_sem, send_sem, recv_sem, out_sem,
):
    rows = n * 8
    samples = f_v.shape[0]
    chunks = f_sem.shape[1]
    width = CELLS // chunks
    me = lax.axis_index("slab")
    barrier = pltpu.get_barrier_semaphore()

    def greet(k, _):
        pl.semaphore_signal(barrier, inc=1, device_id={"slab": lax.rem(me + k, n)}, device_id_type=MESH)
        return 0

    lax.fori_loop(1, n, greet, 0)

    def load(src, dst, sem, b, k):
        at = pl.ds(k * width, width)
        return pltpu.make_async_copy(src.at[b, :, :, at], dst.at[b, :, :, at], sem.at[b, k])

    w_load = pltpu.make_async_copy(mixing, w_v, w_sem)
    for b in range(samples):
        for k in range(chunks):
            load(field, f_v, f_sem, b, k).start()
    w_load.start()
    for b in range(samples):
        for k in range(chunks):
            load(out_grad, o_v, o_sem, b, k).start()

    build_columns(kept_c[0:1, :], t_c, rows)

    turn = signed_x(iota((KX, NX), 0)) * x_of(iota((KX, NX), 1), n, planes)
    to_modes = jnp.concatenate([jnp.cos(turns(turn)), jnp.sin(turns(turn))], axis=0)
    turn = signed_x(iota((NX, KX), 1)) * x_of(iota((NX, KX), 0), n, planes)
    to_lines = jnp.concatenate([jnp.cos(turns(turn)), jnp.sin(turns(turn))], axis=0)
    sign = jnp.where(iota((KX, LANES), 1) < C, 1.0, -1.0).astype(F32)
    sign_x = jnp.where(iota((NX, LANES), 1) < C, -1.0, 1.0).astype(F32)

    def factor(j):
        kept = kept_s[me * owned + j]
        return jnp.where(lax.rem(kept, KZ) > 0, 2.0, 1.0).astype(F32) * SCALE

    factors = [factor(j) for j in range(owned)]

    def exchange(phase, b):
        def go(k, _):
            to = lax.rem(me + k, n)
            pltpu.make_async_remote_copy(
                src_ref=send.at[phase, b, to],
                dst_ref=recv.at[phase, b, me],
                send_sem=send_sem.at[phase, b],
                recv_sem=recv_sem.at[phase, b],
                device_id={"slab": to},
                device_id_type=MESH,
            ).start()
            return 0

        lax.fori_loop(1, n, go, 0)
        recv[phase, b, me] = send[phase, b, me]

    def arrive(phase, b):
        part = recv.at[phase, b, pl.ds(0, n - 1)]
        pltpu.make_async_copy(part, part, recv_sem.at[phase, b]).wait()

    def spread(phase, b):
        store[...] = acc[...].T.reshape(n, 8, planes * C)
        for x in range(planes):
            pieces = [store[:, g, pl.ds(x * C, C)] for g in range(2 * owned)]
            send[phase, b, :, x, :] = jnp.concatenate(pieces, axis=1)

    def plane_products(v, at):
        hi, lo = split(v)
        first = dot(hi, t_c[at, :])
        return first[:, :rows] + first[:, rows:] + dot(lo, t_c[at, pl.ds(0, rows)])

    def forward_field(b):
        for k in range(chunks):
            load(field, f_v, f_sem, b, k).wait()
            v = f_v[b, :, :, pl.ds(k * width, width)].reshape(planes * C, width)
            got = plane_products(v, pl.ds(k * width, width))
            acc[...] = got if k == 0 else acc[...] + got

    def received_modes(phase, b):
        lines = jnp.concatenate([recv[phase, b, :, x, :] for x in range(planes)], axis=0)
        both = jnp.dot(to_modes, lines, preferred_element_type=F32, precision=HIGH)
        out = []
        for j in range(owned):
            at = slice(j * LANES, (j + 1) * LANES)
            out.append(both[:KX, at] + swap(both[KX:, at]) * sign)
        return out

    def total(at, first):
        out = res[at, first, :]
        for r in range(first + 1, first + 8):
            out = out + res[at, r, :]
        return out

    def fold(v):
        return v.reshape(C // 8, 8, LANES).sum(axis=0)

    def send_lines(phase, b, modes):
        modes = jnp.concatenate(modes, axis=1)
        both = jnp.dot(to_lines, modes, preferred_element_type=F32, precision=HIGH)
        out = []
        for j in range(owned):
            at = slice(j * LANES, (j + 1) * LANES)
            out.append(both[:NX, at] + swap(both[NX:, at]) * sign_x)
        lines = jnp.concatenate(out, axis=1)
        for x in range(planes):
            send[phase, b, :, x, :] = lines[x * n : (x + 1) * n, :]
        exchange(phase, b)

    def mix(b):
        for j, modes in enumerate(received_modes(0, b)):
            mid[0, j, b] = modes * SCALE

        def body(j, _):
            lhs = turned(mid[0, j, b])
            for start in range(0, KX, 4):
                wide = dot(lhs, e_mix[:, start * LANES : (start + 4) * LANES])
                for a in range(4):
                    at = j * KX + start + a
                    w = w_v[at]
                    m = wide[:, a * LANES : (a + 1) * LANES]
                    res[at, 0:8, :] = fold(w * m[:C])
                    res[at, 8:16, :] = fold(w * m[C:])
            return 0

        lax.fori_loop(0, owned, body, 0)
        out = []
        for j in range(owned):
            at = pl.ds(j * KX, KX)
            out.append((total(at, 0) - swap(total(at, 8)) * sign) * factors[j])
        send_lines(1, b, out)

    def unmix(b):
        for j, grads in enumerate(received_modes(2, b)):
            mid[1, j, b] = grads * factors[j]
        half = KX // 2

        def body(j, _):
            lhs = turned(mid[1, j, b])
            for start in range(0, half, 4):
                wide = dot(lhs, e_unmix[:, start * LANES : (start + 4) * LANES])
                for a in range(4):
                    at = j * half + start + a
                    w_re, w_im = w_t[at, :C, :], w_t[at, C:, :]
                    g = wide[:, a * LANES : (a + 1) * LANES]
                    res[at, 0:8, :] = fold(w_re * g[:C] + w_im * g[C:])
                    res[at, 8:16, :] = fold(w_re * g[C:] - w_im * g[:C])
            return 0

        lax.fori_loop(0, owned, body, 0)
        out = []
        low_h = iota((half, LANES), 1) < C
        for j in range(owned):
            at = pl.ds(j * half, half)
            real, imag = total(at, 0), total(at, 8)
            early = jnp.where(low_h, real, swap(imag))
            late = jnp.where(low_h, swap(real), imag)
            out.append(jnp.concatenate([early, late], axis=0) * SCALE)
        send_lines(3, b, out)

    def through_cells(b):
        first = lines_matrix(recv.at[1], b, store, n, planes, owned)
        for k in range(chunks):
            load(out_grad, o_v, o_sem, b, k).wait()
        step = pipe.shape[3]

        def add(slot, k):
            at = pl.ds(pl.multiple_of(k * step, step), step)
            got = dot(pipe[slot, 0], t_c[at, :])
            acc[...] += got[:, :rows] + got[:, rows:] + dot(pipe[slot, 1], t_c[at, pl.ds(0, rows)])

        def cells(slot, k):
            at = pl.ds(pl.multiple_of(k * step, step), step)
            pre = dot(first, t_r[:, at])
            v = o_v[b, :, :, at].reshape(planes * C, step) * gelu_slope(pre)
            hi, lo = split(v)
            pipe[slot, 0] = hi
            pipe[slot, 1] = lo

        def body(i, _):
            add(1, jnp.maximum(2 * i - 1, 0))
            cells(0, 2 * i)
            add(0, 2 * i)
            cells(1, 2 * i + 1)
            return 0

        acc[...] = jnp.zeros_like(acc)
        pipe[1] = jnp.zeros(pipe.shape[1:], BF16)
        lax.fori_loop(0, CELLS // step // 2, body, 0)
        add(1, CELLS // step - 1)

    forward_field(0)
    spread(0, 0)
    pl.semaphore_wait(barrier, n - 1)
    exchange(0, 0)
    for b in range(1, samples):
        forward_field(b)
        spread(0, b)
        exchange(0, b)

    build_rows(kept_r[...], t_r, rows)
    build_spread(e_mix, False)
    w_load.wait()

    for b in range(samples):
        arrive(0, b)
        mix(b)

    build_spread(e_unmix, True)

    def turn_over(j, _):
        for p in range(KX // 2):
            at = j * KX + p
            w_t[j * (KX // 2) + p] = jnp.concatenate([w_v[at], w_v[at + KX // 2]], axis=0).T
        return 0

    lax.fori_loop(0, owned, turn_over, 0)

    store[...] = jnp.zeros_like(store)
    for b in range(samples):
        arrive(1, b)
        through_cells(b)
        spread(2, b)
        exchange(2, b)
    for b in range(samples):
        arrive(2, b)
        unmix(b)
    outs = [
        pltpu.make_async_copy(mid.at[0], modes_out, out_sem.at[0]),
        pltpu.make_async_copy(mid.at[1], grads_out, out_sem.at[1]),
    ]
    for copy in outs:
        copy.start()
    for b in range(samples):
        arrive(3, b)
    outs.append(pltpu.make_async_copy(recv.at[3], lines_out, out_sem.at[2]))
    outs[2].start()
    for copy in outs:
        copy.wait()
    for phase in range(4):
        for b in range(samples):
            part = send.at[phase, b, pl.ds(0, n - 1)]
            pltpu.make_async_copy(part, part, send_sem.at[phase, b]).wait()


def last_kernel(
    n, planes, owned,
    kept_r, modes, grads, lines,
    gm_out, gf_out,
    t_r, store, e_mix, gm, gf, gm_sem, gf_sem,
):
    rows = n * 8
    samples = gf.shape[0]
    sign = jnp.where(iota((KX, LANES), 1) < C, 1.0, -1.0).astype(F32)

    build_spread(e_mix, False)

    def weights(j):
        at = pl.ds(j * KX, KX)
        return pltpu.make_async_copy(gm.at[at], gm_out.at[at], gm_sem.at[j])

    def outer(j, _):
        parts = []
        for b in range(samples):
            g = grads[j, b]
            parts.append((turned(modes[j, b]), g, swap(g) * sign))
        for start in range(0, KX, 4):
            wide = [dot(lhs, e_mix[:, start * LANES : (start + 4) * LANES]) for lhs, _, _ in parts]
            for r in range(4):
                a = start + r
                got = None
                for u, (_, g, g_swap) in zip(wide, parts):
                    u = u[:, r * LANES : (r + 1) * LANES]
                    term = u[:C] * g[a : a + 1, :] + u[C:] * g_swap[a : a + 1, :]
                    got = term if got is None else got + term
                gm[j * KX + a] = got
        weights(j).start()
        return 0

    lax.fori_loop(0, owned, outer, 0)

    build_rows(kept_r[...], t_r, rows)
    store[...] = jnp.zeros_like(store)
    chunks = gf_sem.shape[1]
    width = CELLS // chunks
    for b in range(samples):
        first = lines_matrix(lines, b, store, n, planes, owned)

        def chunk_of(k, b=b):
            at = pl.ds(pl.multiple_of(k * width, width), width)
            return at, pltpu.make_async_copy(gf.at[b, :, :, at], gf_out.at[b, :, :, at], gf_sem.at[b, k])

        def body(k, _):
            at, copy = chunk_of(k)
            out = dot(first, t_r[:, at])
            gf[b, :, :, at] = out.reshape(planes, C, width)
            copy.start()
            return 0

        lax.fori_loop(0, chunks, body, 0)
    for j in range(owned):
        weights(j).wait()
    for b in range(samples):
        def done(k, _, b=b):
            at = pl.ds(pl.multiple_of(k * width, width), width)
            pltpu.make_async_copy(gf.at[b, :, :, at], gf_out.at[b, :, :, at], gf_sem.at[b, k]).wait()
            return 0

        lax.fori_loop(0, chunks, done, 0)


def on_device(n, field, out_grad, kept, mixing):
    samples, planes = field.shape[:2]
    owned = mixing.shape[0]
    rows = n * 8
    kept = kept.astype(jnp.int32)
    each = jnp.broadcast_to(kept.reshape(n, owned, 1), (n, owned, 2)).reshape(n, 2 * owned)
    each = jnp.pad(each, ((0, 0), (0, 8 - 2 * owned)), constant_values=-1).reshape(rows)
    kept_r = jnp.broadcast_to(each[:, None], (rows, LANES))
    kept_c = jnp.broadcast_to(each[None, :], (8, rows))
    vmem = pl.BlockSpec(memory_space=pltpu.VMEM)
    hbm = pl.BlockSpec(memory_space=pl.ANY)
    smem = pl.BlockSpec(memory_space=pltpu.SMEM)
    chunks = 8
    block = (n, planes, owned * LANES)
    modes, grads, lines = pl.pallas_call(
        functools.partial(main_kernel, n, planes, owned),
        out_shape=[
            jax.ShapeDtypeStruct((owned, samples, KX, LANES), F32),
            jax.ShapeDtypeStruct((owned, samples, KX, LANES), F32),
            jax.ShapeDtypeStruct((samples,) + block, F32),
        ],
        in_specs=[smem, vmem, vmem, hbm, hbm, hbm],
        out_specs=[hbm, hbm, hbm],
        scratch_shapes=[
            pltpu.VMEM(field.shape, F32),
            pltpu.VMEM(field.shape, F32),
            pltpu.VMEM((owned * KX, C, LANES), F32),
            pltpu.VMEM((owned * KX // 2, LANES, LANES), F32),
            pltpu.VMEM((3 * rows, CELLS), BF16),
            pltpu.VMEM((CELLS, 2 * rows), BF16),
            pltpu.VMEM((planes * C, rows), F32),
            pltpu.VMEM((n, 8, planes * C), F32),
            pltpu.VMEM((2, 2, planes * C, 256), BF16),
            pltpu.VMEM((2 * KX, KX * LANES), BF16),
            pltpu.VMEM((2 * KX, KX * LANES // 2), BF16),
            pltpu.VMEM((owned * KX, 16, LANES), F32),
            pltpu.VMEM((2, owned, samples, KX, LANES), F32),
            pltpu.VMEM((4, samples) + block, F32),
            pltpu.VMEM((4, samples) + block, F32),
            pltpu.SemaphoreType.DMA((samples, chunks)),
            pltpu.SemaphoreType.DMA((samples, chunks)),
            pltpu.SemaphoreType.DMA,
            pltpu.SemaphoreType.DMA((4, samples)),
            pltpu.SemaphoreType.DMA((4, samples)),
            pltpu.SemaphoreType.DMA((3,)),
        ],
        compiler_params=pltpu.CompilerParams(
            collective_id=0, has_side_effects=True, vmem_limit_bytes=56 * 2**20
        ),
    )(kept, kept_r, kept_c, field, out_grad, mixing.reshape(owned * KX, C, LANES))
    grad_mixing, grad_field = pl.pallas_call(
        functools.partial(last_kernel, n, planes, owned),
        out_shape=[
            jax.ShapeDtypeStruct((owned * KX, C, LANES), F32),
            jax.ShapeDtypeStruct(field.shape, F32),
        ],
        in_specs=[vmem, vmem, vmem, vmem],
        out_specs=[hbm, hbm],
        scratch_shapes=[
            pltpu.VMEM((3 * rows, CELLS), BF16),
            pltpu.VMEM((n, 8, planes * C), F32),
            pltpu.VMEM((2 * KX, KX * LANES), BF16),
            pltpu.VMEM((owned * KX, C, LANES), F32),
            pltpu.VMEM(field.shape, F32),
            pltpu.SemaphoreType.DMA((owned,)),
            pltpu.SemaphoreType.DMA((samples, chunks)),
        ],
        compiler_params=pltpu.CompilerParams(vmem_limit_bytes=56 * 2**20),
    )(kept_r, modes, grads, lines)
    return grad_mixing.reshape(mixing.shape), grad_field


def solution(mesh):
    n = mesh.shape["slab"]
    placed = (
        P("group", "slab", None, None),
        P("group", "slab", None, None),
        P(),
        P("slab", None, None, None),
    )
    return jax.shard_map(
        functools.partial(on_device, n),
        mesh=mesh,
        in_specs=placed,
        out_specs=(P(("group", "slab"), None, None, None), P("group", "slab", None, None)),
        check_vma=False,
    )
```
